1024 devices in a mesh: fsdp: 16 (over y_lo, x), tensor: 64 (over z, y_hi, core).
Axes of the slice: x: 4, y: 8 (y_hi: 2, y_lo: 4; y = y_hi * 4 + y_lo), z: 16, core: 2. Of those that a mesh axis runs over, the one named last changes fastest.
Arguments:
- tokens: bfloat16 [4096, 8192], P(('fsdp', 'tensor')), may hold values from -6 to 6
- weight_codes: bfloat16 [8192, 8192], P('fsdp', 'tensor'), may hold values from -6 to 6
- block_scales: bfloat16 [64, 64], P('fsdp', 'tensor'), may hold values from 0.0049743652 to 0.024902344
- grad_out: bfloat16 [4096, 8192], P('fsdp', 'tensor'), may hold values from -0.119628906 to 0.119628906
Outputs:
- projected: bfloat16 [4096, 8192], P('fsdp', 'tensor')
- weight_grad: bfloat16 [8192, 8192], P('fsdp', 'tensor')
The draws below stay inside these ranges and needn't reach their ends.
All inputs are finite; a program needn't handle non-finite values.
Results may differ from the reference program's by a relative error of at most 0.0049.
Values may be sent and summed in bfloat16 or wider, within the bound.
A program may use at most 32 MiB of HBM per device.

```python
import math
import jax
import jax.numpy as jnp
from jax import lax

D = 8192
BLOCK = 128
TOK_GRP = 256
COLS = 8192
TOKENS = 4096
N_FSDP = 16


def level_of(rng, shape, shards, smallest, largest):
    gain, own = 1.0, jax.random.fold_in(rng, 6)
    for position, blocks in shards:
        draws = jnp.exp(jax.random.uniform(jax.random.fold_in(own, position), (blocks,), jnp.float32, smallest / len(shards), largest / len(shards)))
        gain = gain * jnp.repeat(draws, shape[position] // blocks).reshape([-1 if axis == position else 1 for axis in range(len(shape))])
    return gain


def bell_draw(own_key, extent, width, bound, pieces=(), dtype=jnp.bfloat16):
    factor_of = level_of(own_key, extent, pieces, -0.22, 0.18) if pieces else 1.0
    result = jax.random.normal(own_key, extent, jnp.float32) * width * factor_of
    return jnp.minimum(jnp.maximum(result, -bound), bound).astype(dtype)


def setup_inputs(seed: int = 0) -> dict:
    keys = jax.random.split(jax.random.key(seed), 5)
    return {
        "tokens": bell_draw(keys[0], (TOKENS, D), 1.0, 6.0, ((0, 1024),)),
        "weight_codes": bell_draw(keys[1], (D, COLS), 1.0, 6.0, ((0, 16), (1, 64))),
        "block_scales": jnp.clip(jnp.exp(math.log(0.024902344) - 1.61066415 * jax.random.uniform(keys[2], (D // BLOCK, COLS // BLOCK), jnp.float32) ** level_of(keys[2], (D // BLOCK, COLS // BLOCK), ((0, 16), (1, 64)), -0.2, 0.2)), 0.0049743652, 0.024902344).astype(jnp.bfloat16),
        "grad_out": bell_draw(keys[3], (TOKENS, COLS), 0.02, 0.119628906, ((0, 16), (1, 64))),
    }


def dequantize(weight_codes, block_scales):
    expanded = jnp.repeat(jnp.repeat(block_scales.astype(jnp.float32), BLOCK, axis=0), BLOCK, axis=1)
    return (weight_codes.astype(jnp.float32) * expanded).astype(jnp.bfloat16)


def reference(tokens, weight_codes, block_scales, grad_out):
    weight = lax.optimization_barrier(dequantize(weight_codes, block_scales)).astype(jnp.float32)
    projected = jnp.dot(tokens.astype(jnp.float32), weight, precision=lax.Precision.HIGHEST).astype(jnp.bfloat16)
    token_groups = tokens.reshape(N_FSDP, TOK_GRP, D)
    grad_groups = grad_out.reshape(N_FSDP, TOK_GRP, COLS)

    def add_group(accumulated, group_pair):
        partial_grad = jnp.dot(group_pair[0].astype(jnp.float32).T, group_pair[1].astype(jnp.float32), precision=lax.Precision.HIGHEST)
        return accumulated + partial_grad, None

    accumulated, _ = lax.scan(add_group, jnp.zeros((D, COLS), jnp.float32), (token_groups, grad_groups))
    return projected, accumulated.astype(jnp.bfloat16)
```

```python
import jax
import jax.numpy as jnp
from jax import lax
from jax.experimental import pallas as pl
from jax.experimental.pallas import tpu as pltpu
from jax.sharding import PartitionSpec as P

MESH = pl.DeviceIdType.MESH
NX, NY, NZ, YL = 4, 8, 16, 4
SUB = 2
B16, F32 = jnp.bfloat16, jnp.float32

GROUPS = ((0, 1, -1, 2), (-2, 3, -3, 4), (-4, 5, -5, 6), (-6, 7, -7, -8))
FORWARD = {0: (1,), 1: (2,), 2: (3,), 3: (4,), 4: (5,), 5: (6,), 6: (7,), 7: (8,), 8: ()}
Z_STEPS = sorted({b - a for a, bs in FORWARD.items() for b in bs})
SWAPS = [(dy, dc) for dy in range(NY) for dc in range(2) if dy or dc]


def at(x, y, z, c):
    return ((y % YL) * NX + x, z * 4 + (y // YL) * 2 + c)


def kernel(
    tok, codes, scales, grad, out_p, out_w,
    s32, s16, a16, t32, t16, ws, wg, gg, ps, rp, dd, ds, rd, es, rw,
    a_s, a_r, w_s, w_r, v_s, v_r, g_s, g_r, z_s, z_r, c_s, c_r, p_s, p_r, d_s, d_r, e_s, e_r,
):
    f, t = lax.axis_index("fsdp"), lax.axis_index("tensor")
    x, y, z, c = f % NX, (t // 2) % 2 * YL + f // NX, t // 4, t % 2
    sent = []

    def send(src, dst, send_sem, recv_sem, device):
        copy = pltpu.make_async_remote_copy(
            src_ref=src, dst_ref=dst, send_sem=send_sem, recv_sem=recv_sem,
            device_id=device, device_id_type=MESH,
        )
        copy.start()
        sent.append(copy)
        return copy

    barrier = pltpu.get_barrier_semaphore()
    partners = [at(x, (y + dy) % NY, z, (c + dc) % 2) for dy, dc in SWAPS]
    partners += [at((x + dx) % NX, y, z, c) for dx in range(1, NX)]
    partners += [at(x, y, (z + dz) % NZ, c) for s in Z_STEPS for dz in (s, NZ - s)]
    for device in partners:
        pl.semaphore_signal(barrier, inc=1, device_id=device, device_id_type=MESH)

    rows = tok[...].astype(F32)
    for dest in range(2 * NY):
        yy, cc = dest // 2, dest % 2
        for j in range(NX):
            b = ((yy + 2) % YL) * 16 + j * 4 + (yy // YL) * 2 + cc
            s32[dest, j * 4 : j * 4 + 4, :] = rows[:, b * 128 : b * 128 + 128]
    s16[...] = s32[...].astype(B16)
    scale = scales[...].astype(F32)
    for b in range(4):
        block = codes[b * 128 : b * 128 + 128, :].astype(F32) * scale[b : b + 1, 0:1]
        ws[b // 2, (b % 2) * 128 : (b % 2) * 128 + 128, :] = block.astype(B16)

    pl.semaphore_wait(barrier, len(partners))

    me = y * 2 + c
    swaps = []
    for k, (dy, dc) in enumerate(SWAPS):
        yy, cc = (y + dy) % NY, (c + dc) % 2
        swaps.append(
            send(s16.at[yy * 2 + cc], a16.at[me], a_s.at[k], a_r.at[k], at(x, yy, z, cc))
        )
    a16[me] = s16[me]
    w_in = []
    for k, e in enumerate((2, 6)):
        yy = (y + e) % NY
        w_in.append(
            send(ws.at[yy // YL], wg.at[x, y // YL], w_s.at[k], w_r.at[k], at(x, yy, z, c))
        )

    for copy in swaps:
        copy.wait_recv()
    for src in range(2 * NY):
        yy, cc = src // 2, src % 2
        piece = a16[src].astype(F32)
        for j in range(NX):
            r = ((yy // YL) * 2 + cc) * 4
            t32[yy % YL, r : r + 4, j * 128 : j * 128 + 128] = piece[j * 4 : j * 4 + 4, :]
    t16[0, c] = t32[...].astype(B16)

    z_in, c_in = {}, {}

    def part(d, s):
        n = YL // SUB
        return t16.at[d % NZ, c, s * n : s * n + n]

    def forward(d, s):
        ways = (1, -1) if d == 0 else ((1,) if d < 0 else (-1,))
        for way in ways:
            for far in FORWARD[abs(d)]:
                if far == NZ // 2 and way < 0:
                    continue
                to = -way * far
                step = to - d
                z_in[to, s] = send(
                    part(d, s), part(to, s), z_s.at[to % NZ, s], z_r.at[to % NZ, s],
                    at(x, y, (z - step) % NZ, c),
                )
        c_in[d, s] = send(
            part(d, s), part(d, s), c_s.at[d % NZ, s], c_r.at[d % NZ, s], at(x, y, z, 1 - c)
        )

    def arrive(d):
        for s in range(SUB):
            z_in[d, s].wait_recv()
            forward(d, s)

    for s in range(SUB):
        forward(0, s)

    g_in = []
    for dy in range(1, NY):
        yy = (y + dy) % NY
        g_in.append(send(grad, gg.at[y], g_s.at[dy], g_r.at[dy], at(x, yy, z, c)))
    gg[y] = grad[...]

    def gathered(group):
        rows = []
        for d in group:
            a = t16[d % NZ, 0].reshape(64, 512)
            b = t16[d % NZ, 1].reshape(64, 512)
            rows.append(jnp.concatenate([a, b], axis=1))
        return jnp.concatenate(rows, axis=0)

    def settle(group):
        for d in group:
            for s in range(SUB):
                c_in[d, s].wait_recv()

    p_in = []

    def project(i):
        group = GROUPS[i]
        weight = jnp.concatenate(
            [
                jnp.concatenate([wg[j, 0, h * 128 : h * 128 + 128, :], wg[j, 1, h * 128 : h * 128 + 128, :]], axis=1)
                for h in range(2)
                for j in range(NX)
            ],
            axis=0,
        )
        part_p = jnp.dot(gathered(group), weight, preferred_element_type=F32).astype(B16)
        for n in range(len(group)):
            for yy in range(NY):
                r, q = n * 64 + (yy % YL) * 16, yy // YL
                ps[i, yy, n * 16 : n * 16 + 16, :] = part_p[r : r + 16, q * 128 : q * 128 + 128]
        rp[i, y] = ps[i, y]
        for dy in range(1, NY):
            yy = (y + dy) % NY
            p_in.append(
                send(ps.at[i, yy], rp.at[i, y], p_s.at[i, dy], p_r.at[i, dy], at(x, yy, z, c))
            )

    def gradient(i):
        group = GROUPS[i]
        cot = []
        for d in group:
            first = pl.multiple_of(((z + d + NZ) % NZ) * 16, 16)
            for yl in range(YL):
                cot.append(
                    jnp.concatenate(
                        [gg[yl, pl.ds(first, 16), :], gg[YL + yl, pl.ds(first, 16), :]], axis=1
                    )
                )
        cot = jnp.concatenate(cot, axis=0)
        part_w = lax.dot_general(
            gathered(group), cot, (((0,), (0,)), ((), ())), preferred_element_type=F32
        )
        for q in range(2):
            for h in range(2):
                for j in range(NX):
                    r = (h * NX + j) * 128
                    value = part_w[r : r + 128, q * 128 : q * 128 + 128]
                    if i:
                        value = value + dd[q, j, h]
                    dd[q, j, h] = value

    v_in = []
    arrive(-1)
    arrive(1)
    arrive(-2)
    arrive(2)
    for copy in w_in:
        copy.wait_recv()
    for dx in range(1, NX):
        v_in.append(
            send(wg.at[x], wg.at[x], v_s.at[dx], v_r.at[dx], at((x + dx) % NX, y, z, c))
        )
    arrive(-3)
    arrive(3)
    arrive(-4)
    arrive(4)
    for copy in v_in:
        copy.wait_recv()
    settle(GROUPS[0])
    project(0)
    arrive(-5)
    arrive(5)
    settle(GROUPS[1])
    project(1)
    arrive(-6)
    arrive(6)
    for copy in g_in:
        copy.wait_recv()
    gradient(0)
    arrive(-7)
    arrive(7)
    settle(GROUPS[2])
    gradient(1)
    project(2)
    arrive(-8)
    gradient(2)
    settle(GROUPS[3])
    gradient(3)

    d_in = []
    for k, e in enumerate((2, 6)):
        q = ((y + e) % NY) // YL
        ds[k] = dd[q].astype(B16)
        for dx in range(1, NX):
            xx = (x + dx) % NX
            d_in.append(
                send(ds.at[k, xx], rd.at[k, dx - 1], d_s.at[k, dx], d_r.at[k, dx], at(xx, y, z, c))
            )
    project(3)
    e_in = []
    for k, e in enumerate((2, 6)):
        yy = (y + e) % NY
        q = yy // YL
        total = dd[q, x]
        for dx in range(1, NX):
            d_in[k * (NX - 1) + dx - 1].wait_recv()
            total = total + rd[k, dx - 1].astype(F32)
        es[k] = total.astype(B16)
        e_in.append(
            send(es.at[k], rw.at[y // YL], e_s.at[k], e_r.at[k], at(x, yy, z, c))
        )

    for copy in p_in:
        copy.wait_recv()
    for i, group in enumerate(GROUPS):
        total = rp[i, 0].astype(F32)
        for yy in range(1, NY):
            total = total + rp[i, yy].astype(F32)
        total = total.astype(B16)
        for n, d in enumerate(group):
            first = pl.multiple_of(((z + d + NZ) % NZ) * 16, 16)
            out_p[pl.ds(first, 16), :] = total[n * 16 : n * 16 + 16, :]

    for copy in e_in:
        copy.wait_recv()
    for h in range(2):
        for b in range(2):
            r = (h * 2 + b) * 128
            out_w[r : r + 128, :] = rw[h, b]
    for copy in sent:
        copy.wait_send()


def per_device(tokens, weight_codes, block_scales, grad_out):
    vmem = pl.BlockSpec(memory_space=pltpu.VMEM)
    dma = pltpu.SemaphoreType.DMA
    return pl.pallas_call(
        kernel,
        out_shape=(
            jax.ShapeDtypeStruct((256, 128), B16),
            jax.ShapeDtypeStruct((512, 128), B16),
        ),
        in_specs=[vmem] * 4,
        out_specs=(vmem, vmem),
        scratch_shapes=[
            pltpu.VMEM((16, 16, 128), F32),
            pltpu.VMEM((16, 16, 128), B16),
            pltpu.VMEM((16, 16, 128), B16),
            pltpu.VMEM((YL, 16, 512), F32),
            pltpu.VMEM((NZ, 2, YL, 16, 512), B16),
            pltpu.VMEM((2, 256, 128), B16),
            pltpu.VMEM((NX, 2, 256, 128), B16),
            pltpu.VMEM((NY, 256, 128), B16),
            pltpu.VMEM((4, NY, 64, 128), B16),
            pltpu.VMEM((4, NY, 64, 128), B16),
            pltpu.VMEM((2, NX, 2, 128, 128), F32),
            pltpu.VMEM((2, NX, 2, 128, 128), B16),
            pltpu.VMEM((2, NX - 1, 2, 128, 128), B16),
            pltpu.VMEM((2, 2, 128, 128), B16),
            pltpu.VMEM((2, 2, 128, 128), B16),
            dma((15,)), dma((15,)),
            dma((2,)), dma((2,)),
            dma((NX,)), dma((NX,)),
            dma((NY,)), dma((NY,)),
            dma((NZ, SUB)), dma((NZ, SUB)),
            dma((NZ, SUB)), dma((NZ, SUB)),
            dma((4, NY)), dma((4, NY)),
            dma((2, NX)), dma((2, NX)),
            dma((2,)), dma((2,)),
        ],
        compiler_params=pltpu.CompilerParams(
            collective_id=0, has_side_effects=True, vmem_limit_bytes=48 << 20
        ),
    )(tokens, weight_codes, block_scales, grad_out)


def solution(mesh):
    spec = P("fsdp", "tensor")
    return jax.shard_map(
        per_device,
        mesh=mesh,
        in_specs=(P(("fsdp", "tensor"), None), spec, spec, spec),
        out_specs=(spec, spec),
        check_vma=False,
    )
```

```python
import jax
import jax.numpy as jnp
from jax import lax
from jax.experimental import pallas as pl
from jax.experimental.pallas import tpu as pltpu
from jax.sharding import PartitionSpec as P

MESH = pl.DeviceIdType.MESH
NX, NY, NZ, YL = 4, 8, 16, 4
SUB = 2
B16, F32 = jnp.bfloat16, jnp.float32

GROUPS = ((0, -2, 2, -1, 1), (-4, 4, -3, 3), (-6, 6, -5, 5), (-8, -7, 7))
FIRST = (0, 5, 9, 13)
Z_STEPS = (1, 2)
SWAPS = [(dy, dc) for dy in range(NY) for dc in range(2) if dy or dc]


def at(x, y, z, c):
    return ((y % YL) * NX + x, z * 4 + (y // YL) * 2 + c)


def kernel(
    tok_h, codes_h, scales_h, grad_h, out_p, out_w,
    tok, codes, scales, s32, s16, a16, t32, t16, ws, wg, gg, ps, rp, dd, ds, rd, es, rw, i_s,
    a_s, a_r, w_s, w_r, v_s, v_r, g_s, g_r, z_s, z_r, c_s, c_r, p_s, p_r, d_s, d_r, e_s, e_r,
):
    f, t = lax.axis_index("fsdp"), lax.axis_index("tensor")
    x, y, z, c = f % NX, (t // 2) % 2 * YL + f // NX, t // 4, t % 2
    sent = []

    def send(src, dst, send_sem, recv_sem, device):
        copy = pltpu.make_async_remote_copy(
            src_ref=src, dst_ref=dst, send_sem=send_sem, recv_sem=recv_sem,
            device_id=device, device_id_type=MESH,
        )
        copy.start()
        sent.append(copy)
        return copy

    barrier = pltpu.get_barrier_semaphore()
    partners = [at(x, (y + dy) % NY, z, (c + dc) % 2) for dy, dc in SWAPS]
    partners += [at((x + dx) % NX, y, z, c) for dx in range(1, NX)]
    partners += [at(x, y, (z + dz) % NZ, c) for s in Z_STEPS for dz in (s, NZ - s)]
    for device in partners:
        pl.semaphore_signal(barrier, inc=1, device_id=device, device_id_type=MESH)

    loads = [
        pltpu.make_async_copy(tok_h, tok, i_s.at[0]),
        pltpu.make_async_copy(codes_h, codes, i_s.at[1]),
        pltpu.make_async_copy(scales_h, scales, i_s.at[2]),
        pltpu.make_async_copy(grad_h, gg.at[y], i_s.at[3]),
    ]
    for load in loads:
        load.start()

    loads[0].wait()
    rows = tok[...].astype(F32)
    for dest in range(2 * NY):
        yy, cc = dest // 2, dest % 2
        for j in range(NX):
            b = ((yy + 2) % YL) * 16 + j * 4 + (yy // YL) * 2 + cc
            s32[dest, j * 4 : j * 4 + 4, :] = rows[:, b * 128 : b * 128 + 128]
    s16[...] = s32[...].astype(B16)

    pl.semaphore_wait(barrier, len(partners))

    me = y * 2 + c
    swaps = []
    for k, (dy, dc) in enumerate(SWAPS):
        yy, cc = (y + dy) % NY, (c + dc) % 2
        swaps.append(
            send(s16.at[yy * 2 + cc], a16.at[me], a_s.at[k], a_r.at[k], at(x, yy, z, cc))
        )
    a16[me] = s16[me]

    loads[1].wait()
    loads[2].wait()
    scale = scales[...].astype(F32)
    for b in range(4):
        block = codes[b * 128 : b * 128 + 128, :].astype(F32) * scale[0:1, b : b + 1]
        ws[b // 2, (b % 2) * 128 : (b % 2) * 128 + 128, :] = block.astype(B16)
    loads[3].wait()

    for copy in swaps:
        copy.wait_recv()
    for src in range(2 * NY):
        yy, cc = src // 2, src % 2
        piece = a16[src].astype(F32)
        for j in range(NX):
            r = ((yy // YL) * 2 + cc) * 4
            t32[yy % YL, r : r + 4, j * 128 : j * 128 + 128] = piece[j * 4 : j * 4 + 4, :]
    t16[0, c] = t32[...].astype(B16)

    z_in, c_in = {}, {}

    def part(d, s):
        n = YL // SUB
        return t16.at[d % NZ, c, s * n : s * n + n]

    def hop(d, to, s):
        z_in[to, s] = send(
            part(d, s), part(to, s), z_s.at[to % NZ, s], z_r.at[to % NZ, s],
            at(x, y, (z + NZ + d - to) % NZ, c),
        )

    def swap(d):
        for s in range(SUB):
            c_in[d, s] = send(
                part(d, s), part(d, s), c_s.at[d % NZ, s], c_r.at[d % NZ, s], at(x, y, z, 1 - c)
            )

    def level(n):
        here = (0,) if n == 0 else ((-8,) if n == 4 else (-2 * n, 2 * n))
        ways = [(d, w) for d in here for w in ((-1, 1) if d == 0 else ((-1,) if d < 0 else (1,)))]
        for s in range(SUB):
            for d in here:
                if d:
                    z_in[d, s].wait_recv()
                for e, w in ways:
                    if e == d and abs(d + 2 * w) <= 8 and d + 2 * w != 8:
                        hop(d, d + 2 * w, s)
        for d, w in ways:
            if abs(d) < 8:
                for s in range(SUB):
                    hop(d, d + w, s)
        for d in here:
            swap(d)
        if n:
            for d in (-2 * n + 1, 2 * n - 1):
                for s in range(SUB):
                    z_in[d, s].wait_recv()
                swap(d)

    def settle(i):
        for d in GROUPS[i]:
            for s in range(SUB):
                c_in[d, s].wait_recv()

    def gathered(group):
        rows = []
        for d in group:
            a = t16[d % NZ, 0].reshape(64, 512)
            b = t16[d % NZ, 1].reshape(64, 512)
            rows.append(jnp.concatenate([a, b], axis=1))
        return jnp.concatenate(rows, axis=0)

    p_in = []

    def project(i):
        group = GROUPS[i]
        weight = jnp.concatenate(
            [
                jnp.concatenate([wg[j, 0, h * 128 : h * 128 + 128, :], wg[j, 1, h * 128 : h * 128 + 128, :]], axis=1)
                for h in range(2)
                for j in range(NX)
            ],
            axis=0,
        )
        part_p = jnp.dot(gathered(group), weight, preferred_element_type=F32).astype(B16)
        first, size = FIRST[i] * 16, len(group) * 16
        for n in range(len(group)):
            for yy in range(NY):
                r, q = n * 64 + (yy % YL) * 16, yy // YL
                ps[yy, first + n * 16 : first + n * 16 + 16, :] = part_p[r : r + 16, q * 128 : q * 128 + 128]
        rp[y, first : first + size, :] = ps[y, first : first + size, :]
        for dy in range(1, NY):
            yy = (y + dy) % NY
            p_in.append(
                send(
                    ps.at[yy, first : first + size], rp.at[y, first : first + size],
                    p_s.at[i, dy], p_r.at[i, dy], at(x, yy, z, c),
                )
            )

    def gradient(i):
        group = GROUPS[i]
        cot = []
        for d in group:
            first = pl.multiple_of(((z + d + NZ) % NZ) * 16, 16)
            for yl in range(YL):
                cot.append(
                    jnp.concatenate(
                        [gg[yl, pl.ds(first, 16), :], gg[YL + yl, pl.ds(first, 16), :]], axis=1
                    )
                )
        cot = jnp.concatenate(cot, axis=0)
        part_w = lax.dot_general(
            gathered(group), cot, (((0,), (0,)), ((), ())), preferred_element_type=F32
        )
        for q in range(2):
            for h in range(2):
                for j in range(NX):
                    r = (h * NX + j) * 128
                    value = part_w[r : r + 128, q * 128 : q * 128 + 128]
                    if i:
                        value = value + dd[q, j, h]
                    dd[q, j, h] = value

    level(0)
    w_in, v_in, g_in = [], [], {}
    for k, e in enumerate((2, 6)):
        yy = (y + e) % NY
        w_in.append(
            send(ws.at[yy // YL], wg.at[x, y // YL], w_s.at[k], w_r.at[k], at(x, yy, z, c))
        )
    level(1)

    def cotangent(d, to):
        origin = (y + NY + d) % NY
        g_in[to] = send(
            gg.at[origin], gg.at[origin], g_s.at[to % NY], g_r.at[to % NY], at(x, (y + NY + d - to) % NY, z, c)
        )

    for to in (-2, 2, -1, 1):
        cotangent(0, to)
    for copy in w_in:
        copy.wait_recv()
    for dx in (2, 1, 3):
        v_in.append(
            send(wg.at[x], wg.at[x], v_s.at[dx], v_r.at[dx], at((x + dx) % NX, y, z, c))
        )
    level(2)
    for d, to in ((-2, -4), (-2, -3), (2, 3)):
        if to != -3:
            g_in[d].wait_recv()
        cotangent(d, to)
    level(3)
    for copy in v_in:
        copy.wait_recv()
    settle(0)
    project(0)
    settle(1)
    project(1)
    for to in (-1, 1, -4, -3, 3):
        g_in[to].wait_recv()
    gradient(0)
    gradient(1)
    level(4)
    settle(2)
    gradient(2)
    settle(3)
    gradient(3)

    d_in = {}
    for k, e in enumerate((2, 6)):
        q = ((y + e) % NY) // YL
        ds[k] = dd[q].astype(B16)
        for dx in (2, 1, 3):
            xx = (x + dx) % NX
            d_in[k, dx] = send(
                ds.at[k, xx], rd.at[k, dx - 1], d_s.at[k, dx], d_r.at[k, dx], at(xx, y, z, c)
            )
    project(2)
    project(3)
    e_in = []
    for k, e in enumerate((2, 6)):
        yy = (y + e) % NY
        q = yy // YL
        total = dd[q, x]
        for dx in range(1, NX):
            d_in[k, dx].wait_recv()
            total = total + rd[k, dx - 1].astype(F32)
        es[k] = total.astype(B16)
        e_in.append(
            send(es.at[k], rw.at[y // YL], e_s.at[k], e_r.at[k], at(x, yy, z, c))
        )

    for copy in p_in:
        copy.wait_recv()
    for i, group in enumerate(GROUPS):
        for n, d in enumerate(group):
            r = (FIRST[i] + n) * 16
            total = rp[0, r : r + 16, :].astype(F32)
            for yy in range(1, NY):
                total = total + rp[yy, r : r + 16, :].astype(F32)
            first = pl.multiple_of(((z + d + NZ) % NZ) * 16, 16)
            out_p[pl.ds(first, 16), :] = total.astype(B16)

    for copy in e_in:
        copy.wait_recv()
    for h in range(2):
        for b in range(2):
            r = (h * 2 + b) * 128
            out_w[r : r + 128, :] = rw[h, b]
    for copy in sent:
        copy.wait_send()


def per_device(tokens, weight_codes, block_scales, grad_out):
    vmem = pl.BlockSpec(memory_space=pltpu.VMEM)
    dma = pltpu.SemaphoreType.DMA
    return pl.pallas_call(
        kernel,
        out_shape=(
            pltpu.VMEM((256, 128), B16),
            pltpu.VMEM((512, 128), B16),
        ),
        in_specs=[pl.BlockSpec(memory_space=pltpu.HBM)] * 4,
        out_specs=(vmem, vmem),
        scratch_shapes=[
            pltpu.VMEM((4, 8192), B16),
            pltpu.VMEM((512, 128), B16),
            pltpu.VMEM((1, 4), B16),
            pltpu.VMEM((16, 16, 128), F32),
            pltpu.VMEM((16, 16, 128), B16),
            pltpu.VMEM((16, 16, 128), B16),
            pltpu.VMEM((YL, 16, 512), F32),
            pltpu.VMEM((NZ, 2, YL, 16, 512), B16),
            pltpu.VMEM((2, 256, 128), B16),
            pltpu.VMEM((NX, 2, 256, 128), B16),
            pltpu.VMEM((NY, 256, 128), B16),
            pltpu.VMEM((NY, 256, 128), B16),
            pltpu.VMEM((NY, 256, 128), B16),
            pltpu.VMEM((2, NX, 2, 128, 128), F32),
            pltpu.VMEM((2, NX, 2, 128, 128), B16),
            pltpu.VMEM((2, NX - 1, 2, 128, 128), B16),
            pltpu.VMEM((2, 2, 128, 128), B16),
            pltpu.VMEM((2, 2, 128, 128), B16),
            dma((4,)),
            dma((15,)), dma((15,)),
            dma((2,)), dma((2,)),
            dma((NX,)), dma((NX,)),
            dma((NY,)), dma((NY,)),
            dma((NZ, SUB)), dma((NZ, SUB)),
            dma((NZ, SUB)), dma((NZ, SUB)),
            dma((4, NY)), dma((4, NY)),
            dma((2, NX)), dma((2, NX)),
            dma((2,)), dma((2,)),
        ],
        compiler_params=pltpu.CompilerParams(
            collective_id=0, has_side_effects=True, vmem_limit_bytes=60 << 20
        ),
    )(tokens, weight_codes, block_scales.T, grad_out)


def solution(mesh):
    spec = P("fsdp", "tensor")
    return jax.shard_map(
        per_device,
        mesh=mesh,
        in_specs=(P(("fsdp", "tensor"), None), spec, spec, spec),
        out_specs=(spec, spec),
        check_vma=False,
    )
```

```python
import jax
import jax.numpy as jnp
from jax import lax
from jax.experimental import pallas as pl
from jax.experimental.pallas import tpu as pltpu
from jax.sharding import PartitionSpec as P

MESH = pl.DeviceIdType.MESH
NX, NY, NZ, YL = 4, 8, 16, 4
SUB = 2
B16, F32 = jnp.bfloat16, jnp.float32

GROUPS = ((0, -2, 2, -1, 1), (-4, 4, -3, 3), (-6, 6, -5, 5), (-8, -7, 7))
FIRST = (0, 5, 9, 13)
Z_STEPS = (1, 2)
SWAPS = [(dy, dc) for dy in (4, 3, 5, 2, 6, 1, 7, 0) for dc in range(2) if dy or dc]
PHASES = 4


def at(x, y, z, c):
    return ((y % YL) * NX + x, z * 4 + (y // YL) * 2 + c)


def kernel(
    tok_h, codes_h, scales_h, grad_h, out_p, out_w,
    tok, codes, scales, s32, s16, a16, t32, t16, ws, wg, gg, ps, rp, dd, ds, rd, es, rw, i_s,
    a_s, a_r, w_s, w_r, v_s, v_r, g_s, g_r, z_s, z_r, c_s, c_r, p_s, p_r, d_s, d_r, e_s, e_r,
):
    f, t = lax.axis_index("fsdp"), lax.axis_index("tensor")
    x, y, z, c = f % NX, (t // 2) % 2 * YL + f // NX, t // 4, t % 2
    sent = []

    def send(src, dst, send_sem, recv_sem, device):
        copy = pltpu.make_async_remote_copy(
            src_ref=src, dst_ref=dst, send_sem=send_sem, recv_sem=recv_sem,
            device_id=device, device_id_type=MESH,
        )
        copy.start()
        sent.append(copy)
        return copy

    barrier = pltpu.get_barrier_semaphore()
    partners = [at(x, (y + dy) % NY, z, (c + dc) % 2) for dy, dc in SWAPS]
    partners += [at((x + dx) % NX, y, z, c) for dx in range(1, NX)]
    partners += [at(x, y, (z + dz) % NZ, c) for s in Z_STEPS for dz in (s, NZ - s)]
    for device in partners:
        pl.semaphore_signal(barrier, inc=1, device_id=device, device_id_type=MESH)

    loads = [
        pltpu.make_async_copy(tok_h, tok, i_s.at[0]),
        pltpu.make_async_copy(codes_h, codes, i_s.at[1]),
        pltpu.make_async_copy(scales_h, scales, i_s.at[2]),
        pltpu.make_async_copy(grad_h, gg.at[y], i_s.at[3]),
    ]
    for load in loads:
        load.start()

    loads[0].wait()
    rows = tok[...].astype(F32)
    for dest in range(2 * NY):
        yy, cc = dest // 2, dest % 2
        for j in range(NX):
            b = ((yy + 2) % YL) * 16 + j * 4 + (yy // YL) * 2 + cc
            s32[dest, j * 4 : j * 4 + 4, :] = rows[:, b * 128 : b * 128 + 128]
    s16[...] = s32[...].astype(B16)

    pl.semaphore_wait(barrier, len(partners))

    me = y * 2 + c
    swaps = []
    for k, (dy, dc) in enumerate(SWAPS):
        yy, cc = (y + dy) % NY, (c + dc) % 2
        swaps.append(
            send(s16.at[yy * 2 + cc], a16.at[me], a_s.at[k], a_r.at[k], at(x, yy, z, cc))
        )
    a16[me] = s16[me]

    loads[1].wait()
    loads[2].wait()
    scale = scales[...].astype(F32)
    for b in range(4):
        block = codes[b * 128 : b * 128 + 128, :].astype(F32) * scale[0:1, b : b + 1]
        ws[b // 2, (b % 2) * 128 : (b % 2) * 128 + 128, :] = block.astype(B16)
    loads[3].wait()

    for copy in swaps:
        copy.wait_recv()
    for src in range(2 * NY):
        yy, cc = src // 2, src % 2
        piece = a16[src].astype(F32)
        for j in range(NX):
            r = ((yy // YL) * 2 + cc) * 4
            t32[yy % YL, r : r + 4, j * 128 : j * 128 + 128] = piece[j * 4 : j * 4 + 4, :]
    t16[0, c] = t32[...].astype(B16)

    z_in, c_in = {}, {}

    def part(d, s):
        n = YL // SUB
        return t16.at[d % NZ, c, s * n : s * n + n]

    def hop(d, to, s):
        z_in[to, s] = send(
            part(d, s), part(to, s), z_s.at[to % NZ, s], z_r.at[to % NZ, s],
            at(x, y, (z + NZ + d - to) % NZ, c),
        )

    def swap(d):
        for s in range(SUB):
            c_in[d, s] = send(
                part(d, s), part(d, s), c_s.at[d % NZ, s], c_r.at[d % NZ, s], at(x, y, z, 1 - c)
            )

    def level(n):
        here = (0,) if n == 0 else ((-8,) if n == 4 else (-2 * n, 2 * n))
        ways = [(d, w) for d in here for w in ((-1, 1) if d == 0 else ((-1,) if d < 0 else (1,)))]
        for s in range(SUB):
            for d in here:
                if d:
                    z_in[d, s].wait_recv()
                for e, w in ways:
                    if e == d and abs(d + 2 * w) <= 8 and d + 2 * w != 8:
                        hop(d, d + 2 * w, s)
        for d, w in ways:
            if abs(d) < 8:
                for s in range(SUB):
                    hop(d, d + w, s)
        for d in here:
            swap(d)
        if n:
            for d in (-2 * n + 1, 2 * n - 1):
                for s in range(SUB):
                    z_in[d, s].wait_recv()
                swap(d)

    def settle(i):
        for d in GROUPS[i]:
            for s in range(SUB):
                c_in[d, s].wait_recv()

    def gathered(group):
        rows = []
        for d in group:
            a = t16[d % NZ, 0].reshape(64, 512)
            b = t16[d % NZ, 1].reshape(64, 512)
            rows.append(jnp.concatenate([a, b], axis=1))
        return jnp.concatenate(rows, axis=0)

    p_in = []

    def project(i):
        group = GROUPS[i]
        weight = jnp.concatenate(
            [
                jnp.concatenate([wg[j, 0, h * 128 : h * 128 + 128, :], wg[j, 1, h * 128 : h * 128 + 128, :]], axis=1)
                for h in range(2)
                for j in range(NX)
            ],
            axis=0,
        )
        part_p = jnp.dot(gathered(group), weight, preferred_element_type=F32).astype(B16)
        first, size = FIRST[i] * 16, len(group) * 16
        for n in range(len(group)):
            for yy in range(NY):
                r, q = n * 64 + (yy % YL) * 16, yy // YL
                ps[yy, first + n * 16 : first + n * 16 + 16, :] = part_p[r : r + 16, q * 128 : q * 128 + 128]
        rp[y, first : first + size, :] = ps[y, first : first + size, :]
        for dy in range(1, NY):
            yy = (y + dy) % NY
            p_in.append(
                send(
                    ps.at[yy, first : first + size], rp.at[y, first : first + size],
                    p_s.at[i, dy], p_r.at[i, dy], at(x, yy, z, c),
                )
            )

    def gradient(i):
        group = GROUPS[i]
        cot = []
        for d in group:
            first = pl.multiple_of(((z + d + NZ) % NZ) * 16, 16)
            for yl in range(YL):
                cot.append(
                    jnp.concatenate(
                        [gg[yl, pl.ds(first, 16), :], gg[YL + yl, pl.ds(first, 16), :]], axis=1
                    )
                )
        cot = jnp.concatenate(cot, axis=0)
        part_w = lax.dot_general(
            gathered(group), cot, (((0,), (0,)), ((), ())), preferred_element_type=F32
        )
        for q in range(2):
            for h in range(2):
                for j in range(NX):
                    r = (h * NX + j) * 128
                    value = part_w[r : r + 128, q * 128 : q * 128 + 128]
                    if i:
                        value = value + dd[q, j, h]
                    dd[q, j, h] = value

    level(0)
    w_in, v_in, g_in = [], [], {}
    for k, e in enumerate((2, 6)):
        yy = (y + e) % NY
        w_in.append(
            send(ws.at[yy // YL], wg.at[x, y // YL], w_s.at[k], w_r.at[k], at(x, yy, z, c))
        )
    level(1)

    def cotangent(d, to):
        origin = (y + NY + d) % NY
        g_in[to] = send(
            gg.at[origin], gg.at[origin], g_s.at[to % NY], g_r.at[to % NY], at(x, (y + NY + d - to) % NY, z, c)
        )

    for to in (-2, 2, -1, 1):
        cotangent(0, to)
    for copy in w_in:
        copy.wait_recv()
    for dx in (2, 1, 3):
        v_in.append(
            send(wg.at[x], wg.at[x], v_s.at[dx], v_r.at[dx], at((x + dx) % NX, y, z, c))
        )
    level(2)
    for d, to in ((-2, -4), (-2, -3), (2, 3)):
        if to != -3:
            g_in[d].wait_recv()
        cotangent(d, to)
    level(3)
    for copy in v_in:
        copy.wait_recv()
    settle(0)
    project(0)
    settle(1)
    project(1)
    for to in (-1, 1, -4, -3, 3):
        g_in[to].wait_recv()
    gradient(0)
    gradient(1)
    level(4)
    settle(2)
    gradient(2)
    settle(3)
    gradient(3)

    size = 256 // PHASES
    spans = [(k * size // 128, k * size % 128) for k in range(PHASES)]
    d_in, e_in = {}, []
    for k, (h, r) in enumerate(spans):
        for j in range(NX):
            for q in range(2):
                ds[k, j, q] = dd[q, j, h, r : r + size, :].astype(B16)
        for dx in (2, 1, 3):
            xx = (x + dx) % NX
            d_in[k, dx] = send(
                ds.at[k, xx], rd.at[k, dx - 1], d_s.at[k, dx], d_r.at[k, dx], at(xx, y, z, c)
            )
    project(2)
    project(3)
    for k, (h, r) in enumerate(spans):
        for dx in range(1, NX):
            d_in[k, dx].wait_recv()
        for q in range(2):
            total = dd[q, x, h, r : r + size, :]
            for dx in range(1, NX):
                total = total + rd[k, dx - 1, q].astype(F32)
            es[k, q] = total.astype(B16)
        for i, e in enumerate((2, 6)):
            yy = (y + e) % NY
            e_in.append(
                send(
                    es.at[k, yy // YL], rw.at[y // YL, h, r : r + size],
                    e_s.at[k, i], e_r.at[k, i], at(x, yy, z, c),
                )
            )

    for copy in p_in:
        copy.wait_recv()
    for i, group in enumerate(GROUPS):
        for n, d in enumerate(group):
            r = (FIRST[i] + n) * 16
            total = rp[0, r : r + 16, :].astype(F32)
            for yy in range(1, NY):
                total = total + rp[yy, r : r + 16, :].astype(F32)
            first = pl.multiple_of(((z + d + NZ) % NZ) * 16, 16)
            out_p[pl.ds(first, 16), :] = total.astype(B16)

    for copy in e_in:
        copy.wait_recv()
    for h in range(2):
        for b in range(2):
            r = (h * 2 + b) * 128
            out_w[r : r + 128, :] = rw[h, b]
    for copy in sent:
        copy.wait_send()


def per_device(tokens, weight_codes, block_scales, grad_out):
    vmem = pl.BlockSpec(memory_space=pltpu.VMEM)
    dma = pltpu.SemaphoreType.DMA
    return pl.pallas_call(
        kernel,
        out_shape=(
            pltpu.VMEM((256, 128), B16),
            pltpu.VMEM((512, 128), B16),
        ),
        in_specs=[pl.BlockSpec(memory_space=pltpu.HBM)] * 4,
        out_specs=(vmem, vmem),
        scratch_shapes=[
            pltpu.VMEM((4, 8192), B16),
            pltpu.VMEM((512, 128), B16),
            pltpu.VMEM((1, 4), B16),
            pltpu.VMEM((16, 16, 128), F32),
            pltpu.VMEM((16, 16, 128), B16),
            pltpu.VMEM((16, 16, 128), B16),
            pltpu.VMEM((YL, 16, 512), F32),
            pltpu.VMEM((NZ, 2, YL, 16, 512), B16),
            pltpu.VMEM((2, 256, 128), B16),
            pltpu.VMEM((NX, 2, 256, 128), B16),
            pltpu.VMEM((NY, 256, 128), B16),
            pltpu.VMEM((NY, 256, 128), B16),
            pltpu.VMEM((NY, 256, 128), B16),
            pltpu.VMEM((2, NX, 2, 128, 128), F32),
            pltpu.VMEM((PHASES, NX, 2, 256 // PHASES, 128), B16),
            pltpu.VMEM((PHASES, NX - 1, 2, 256 // PHASES, 128), B16),
            pltpu.VMEM((PHASES, 2, 256 // PHASES, 128), B16),
            pltpu.VMEM((2, 2, 128, 128), B16),
            dma((4,)),
            dma((15,)), dma((15,)),
            dma((2,)), dma((2,)),
            dma((NX,)), dma((NX,)),
            dma((NY,)), dma((NY,)),
            dma((NZ, SUB)), dma((NZ, SUB)),
            dma((NZ, SUB)), dma((NZ, SUB)),
            dma((4, NY)), dma((4, NY)),
            dma((PHASES, NX)), dma((PHASES, NX)),
            dma((PHASES, 2)), dma((PHASES, 2)),
        ],
        compiler_params=pltpu.CompilerParams(
            collective_id=0, has_side_effects=True, vmem_limit_bytes=60 << 20
        ),
    )(tokens, weight_codes, block_scales.T, grad_out)


def solution(mesh):
    spec = P("fsdp", "tensor")
    return jax.shard_map(
        per_device,
        mesh=mesh,
        in_specs=(P(("fsdp", "tensor"), None), spec, spec, spec),
        out_specs=(spec, spec),
        check_vma=False,
    )
```

```python
import jax
import jax.numpy as jnp
from jax import lax
from jax.experimental import pallas as pl
from jax.experimental.pallas import tpu as pltpu
from jax.sharding import PartitionSpec as P

MESH = pl.DeviceIdType.MESH
NX, NY, NZ, YL = 4, 8, 16, 4
SUB = 2
B16, F32 = jnp.bfloat16, jnp.float32

GROUPS = ((0, -2, 2, -1, 1), (-4, 4, -3, 3), (-6, 6, -5, 5), (-8, -7, 7))
FIRST = (0, 5, 9, 13)
Z_STEPS = (1, 2)
SWAPS = [(dy, dc) for dy in (4, 3, 5, 2, 6, 1, 7, 0) for dc in range(2) if dy or dc]
PHASES = 4


def at(x, y, z, c):
    return ((y % YL) * NX + x, z * 4 + (y // YL) * 2 + c)


def kernel(
    tok_h, codes_h, scales_h, grad_h, out_p, out_w,
    tok, codes, scales, s32, s16, a16, t32, t16, ws, wg, gg, ps, rp, dd, ds, rd, es, rw, i_s,
    a_s, a_r, w_s, w_r, v_s, v_r, g_s, g_r, z_s, z_r, c_s, c_r, p_s, p_r, d_s, d_r, e_s, e_r,
):
    f, t = lax.axis_index("fsdp"), lax.axis_index("tensor")
    x, y, z, c = f % NX, (t // 2) % 2 * YL + f // NX, t // 4, t % 2
    sent = []

    def send(src, dst, send_sem, recv_sem, device):
        copy = pltpu.make_async_remote_copy(
            src_ref=src, dst_ref=dst, send_sem=send_sem, recv_sem=recv_sem,
            device_id=device, device_id_type=MESH,
        )
        copy.start()
        sent.append(copy)
        return copy

    barrier = pltpu.get_barrier_semaphore()
    partners = [at(x, (y + dy) % NY, z, (c + dc) % 2) for dy, dc in SWAPS]
    partners += [at((x + dx) % NX, y, z, c) for dx in range(1, NX)]
    partners += [at(x, y, (z + dz) % NZ, c) for s in Z_STEPS for dz in (s, NZ - s)]
    for device in partners:
        pl.semaphore_signal(barrier, inc=1, device_id=device, device_id_type=MESH)

    loads = [
        pltpu.make_async_copy(tok_h, tok, i_s.at[0]),
        pltpu.make_async_copy(codes_h, codes, i_s.at[1]),
        pltpu.make_async_copy(scales_h, scales, i_s.at[2]),
        pltpu.make_async_copy(grad_h, gg.at[y], i_s.at[3]),
    ]
    for load in loads:
        load.start()

    loads[0].wait()
    rows = tok[...].astype(F32)
    for dest in range(2 * NY):
        yy, cc = dest // 2, dest % 2
        for j in range(NX):
            b = ((yy + 2) % YL) * 16 + j * 4 + (yy // YL) * 2 + cc
            s32[dest, j * 4 : j * 4 + 4, :] = rows[:, b * 128 : b * 128 + 128]
    s16[...] = s32[...].astype(B16)

    pl.semaphore_wait(barrier, len(partners))

    me = y * 2 + c
    swaps = []
    for k, (dy, dc) in enumerate(SWAPS):
        yy, cc = (y + dy) % NY, (c + dc) % 2
        swaps.append(
            send(s16.at[yy * 2 + cc], a16.at[me], a_s.at[k], a_r.at[k], at(x, yy, z, cc))
        )
    a16[me] = s16[me]

    loads[1].wait()
    loads[2].wait()
    scale = scales[...].astype(F32)
    for b in range(4):
        block = codes[b * 128 : b * 128 + 128, :].astype(F32) * scale[0:1, b : b + 1]
        ws[b // 2, (b % 2) * 128 : (b % 2) * 128 + 128, :] = block.astype(B16)
    loads[3].wait()

    for copy in swaps:
        copy.wait_recv()
    for src in range(2 * NY):
        yy, cc = src // 2, src % 2
        piece = a16[src].astype(F32)
        for j in range(NX):
            r = ((yy // YL) * 2 + cc) * 4
            t32[yy % YL, r : r + 4, j * 128 : j * 128 + 128] = piece[j * 4 : j * 4 + 4, :]
    t16[0, c] = t32[...].astype(B16)

    z_in, c_in = {}, {}

    def part(d, s):
        n = YL // SUB
        return t16.at[d % NZ, c, s * n : s * n + n]

    def hop(d, to, s):
        z_in[to, s] = send(
            part(d, s), part(to, s), z_s.at[to % NZ, s], z_r.at[to % NZ, s],
            at(x, y, (z + NZ + d - to) % NZ, c),
        )

    def swap(d):
        for s in range(SUB):
            c_in[d, s] = send(
                part(d, s), part(d, s), c_s.at[d % NZ, s], c_r.at[d % NZ, s], at(x, y, z, 1 - c)
            )

    def level(n):
        here = (0,) if n == 0 else ((-8,) if n == 4 else (-2 * n, 2 * n))
        ways = [(d, w) for d in here for w in ((-1, 1) if d == 0 else ((-1,) if d < 0 else (1,)))]
        for s in range(SUB):
            for d in here:
                if d:
                    z_in[d, s].wait_recv()
                for e, w in ways:
                    if e == d and abs(d + 2 * w) <= 8 and d + 2 * w != 8:
                        hop(d, d + 2 * w, s)
        for d, w in ways:
            if abs(d) < 8:
                for s in range(SUB):
                    hop(d, d + w, s)
        for d in here:
            swap(d)
        if n:
            for d in (-2 * n + 1, 2 * n - 1):
                for s in range(SUB):
                    z_in[d, s].wait_recv()
                swap(d)

    def settle(i):
        for d in GROUPS[i]:
            for s in range(SUB):
                c_in[d, s].wait_recv()

    def gathered(group):
        rows = []
        for d in group:
            a = t16[d % NZ, 0].reshape(64, 512)
            b = t16[d % NZ, 1].reshape(64, 512)
            rows.append(jnp.concatenate([a, b], axis=1))
        return jnp.concatenate(rows, axis=0)

    p_in = []

    def project(i):
        group = GROUPS[i]
        weight = jnp.concatenate(
            [
                jnp.concatenate([wg[j, 0, h * 128 : h * 128 + 128, :], wg[j, 1, h * 128 : h * 128 + 128, :]], axis=1)
                for h in range(2)
                for j in range(NX)
            ],
            axis=0,
        )
        part_p = jnp.dot(gathered(group), weight, preferred_element_type=F32).astype(B16)
        first, size = FIRST[i] * 16, len(group) * 16
        for n in range(len(group)):
            for yy in range(NY):
                r, q = n * 64 + (yy % YL) * 16, yy // YL
                ps[yy, first + n * 16 : first + n * 16 + 16, :] = part_p[r : r + 16, q * 128 : q * 128 + 128]
        rp[y, first : first + size, :] = ps[y, first : first + size, :]
        for dy in range(1, NY):
            yy = (y + dy) % NY
            p_in.append(
                send(
                    ps.at[yy, first : first + size], rp.at[y, first : first + size],
                    p_s.at[i, dy], p_r.at[i, dy], at(x, yy, z, c),
                )
            )

    def gradient(i):
        group = GROUPS[i]
        cot = []
        for d in group:
            first = pl.multiple_of(((z + d + NZ) % NZ) * 16, 16)
            for yl in range(YL):
                cot.append(
                    jnp.concatenate(
                        [gg[yl, pl.ds(first, 16), :], gg[YL + yl, pl.ds(first, 16), :]], axis=1
                    )
                )
        cot = jnp.concatenate(cot, axis=0)
        part_w = lax.dot_general(
            gathered(group), cot, (((0,), (0,)), ((), ())), preferred_element_type=F32
        )
        for q in range(2):
            for h in range(2):
                for j in range(NX):
                    r = (h * NX + j) * 128
                    value = part_w[r : r + 128, q * 128 : q * 128 + 128]
                    if i:
                        value = value + dd[q, j, h]
                    dd[q, j, h] = value

    level(0)
    w_in, v_in, g_in = [], [], {}
    for k, e in enumerate((2, 6)):
        yy = (y + e) % NY
        w_in.append(
            send(ws.at[yy // YL], wg.at[x, y // YL], w_s.at[k], w_r.at[k], at(x, yy, z, c))
        )
    level(1)

    def cotangent(d, to):
        origin = (y + NY + d) % NY
        g_in[to] = send(
            gg.at[origin], gg.at[origin], g_s.at[to % NY], g_r.at[to % NY], at(x, (y + NY + d - to) % NY, z, c)
        )

    for to in (-2, 2, -1, 1):
        cotangent(0, to)
    for copy in w_in:
        copy.wait_recv()
    for dx in (2, 1, 3):
        v_in.append(
            send(wg.at[x], wg.at[x], v_s.at[dx], v_r.at[dx], at((x + dx) % NX, y, z, c))
        )
    level(2)
    for d, to in ((-2, -4), (-2, -3), (2, 3)):
        if to != -3:
            g_in[d].wait_recv()
        cotangent(d, to)
    level(3)
    for copy in v_in:
        copy.wait_recv()
    settle(0)
    project(0)
    settle(1)
    project(1)
    for to in (-1, 1, -4, -3, 3):
        g_in[to].wait_recv()
    gradient(0)
    gradient(1)
    settle(2)
    gradient(2)
    level(4)
    settle(3)
    gradient(3)

    size = 256 // PHASES
    spans = [(k * size // 128, k * size % 128) for k in range(PHASES)]
    d_in, e_in = {}, []
    for k, (h, r) in enumerate(spans):
        for j in range(NX):
            for q in range(2):
                ds[k, j, q] = dd[q, j, h, r : r + size, :].astype(B16)
        for dx in (2, 1, 3):
            xx = (x + dx) % NX
            d_in[k, dx] = send(
                ds.at[k, xx], rd.at[k, dx - 1], d_s.at[k, dx], d_r.at[k, dx], at(xx, y, z, c)
            )
    project(2)
    project(3)
    for k, (h, r) in enumerate(spans):
        for dx in range(1, NX):
            d_in[k, dx].wait_recv()
        for q in range(2):
            total = dd[q, x, h, r : r + size, :]
            for dx in range(1, NX):
                total = total + rd[k, dx - 1, q].astype(F32)
            es[k, q] = total.astype(B16)
        for i, e in enumerate((2, 6)):
            yy = (y + e) % NY
            e_in.append(
                send(
                    es.at[k, yy // YL], rw.at[y // YL, h, r : r + size],
                    e_s.at[k, i], e_r.at[k, i], at(x, yy, z, c),
                )
            )

    for copy in p_in:
        copy.wait_recv()
    for i, group in enumerate(GROUPS):
        for n, d in enumerate(group):
            r = (FIRST[i] + n) * 16
            total = rp[0, r : r + 16, :].astype(F32)
            for yy in range(1, NY):
                total = total + rp[yy, r : r + 16, :].astype(F32)
            first = pl.multiple_of(((z + d + NZ) % NZ) * 16, 16)
            out_p[pl.ds(first, 16), :] = total.astype(B16)

    for copy in e_in:
        copy.wait_recv()
    for h in range(2):
        for b in range(2):
            r = (h * 2 + b) * 128
            out_w[r : r + 128, :] = rw[h, b]
    for copy in sent:
        copy.wait_send()


def per_device(tokens, weight_codes, block_scales, grad_out):
    vmem = pl.BlockSpec(memory_space=pltpu.VMEM)
    dma = pltpu.SemaphoreType.DMA
    return pl.pallas_call(
        kernel,
        out_shape=(
            pltpu.VMEM((256, 128), B16),
            pltpu.VMEM((512, 128), B16),
        ),
        in_specs=[pl.BlockSpec(memory_space=pltpu.HBM)] * 4,
        out_specs=(vmem, vmem),
        scratch_shapes=[
            pltpu.VMEM((4, 8192), B16),
            pltpu.VMEM((512, 128), B16),
            pltpu.VMEM((1, 4), B16),
            pltpu.VMEM((16, 16, 128), F32),
            pltpu.VMEM((16, 16, 128), B16),
            pltpu.VMEM((16, 16, 128), B16),
            pltpu.VMEM((YL, 16, 512), F32),
            pltpu.VMEM((NZ, 2, YL, 16, 512), B16),
            pltpu.VMEM((2, 256, 128), B16),
            pltpu.VMEM((NX, 2, 256, 128), B16),
            pltpu.VMEM((NY, 256, 128), B16),
            pltpu.VMEM((NY, 256, 128), B16),
            pltpu.VMEM((NY, 256, 128), B16),
            pltpu.VMEM((2, NX, 2, 128, 128), F32),
            pltpu.VMEM((PHASES, NX, 2, 256 // PHASES, 128), B16),
            pltpu.VMEM((PHASES, NX - 1, 2, 256 // PHASES, 128), B16),
            pltpu.VMEM((PHASES, 2, 256 // PHASES, 128), B16),
            pltpu.VMEM((2, 2, 128, 128), B16),
            dma((4,)),
            dma((15,)), dma((15,)),
            dma((2,)), dma((2,)),
            dma((NX,)), dma((NX,)),
            dma((NY,)), dma((NY,)),
            dma((NZ, SUB)), dma((NZ, SUB)),
            dma((NZ, SUB)), dma((NZ, SUB)),
            dma((4, NY)), dma((4, NY)),
            dma((PHASES, NX)), dma((PHASES, NX)),
            dma((PHASES, 2)), dma((PHASES, 2)),
        ],
        compiler_params=pltpu.CompilerParams(
            collective_id=0, has_side_effects=True, vmem_limit_bytes=60 << 20
        ),
    )(tokens, weight_codes, block_scales.T, grad_out)


def solution(mesh):
    spec = P("fsdp", "tensor")
    return jax.shard_map(
        per_device,
        mesh=mesh,
        in_specs=(P(("fsdp", "tensor"), None), spec, spec, spec),
        out_specs=(spec, spec),
        check_vma=False,
    )
```
